768 devices in a mesh: face: 96 (over z, y), tile: 8 (over x, core).
Axes of the slice: x: 4, y: 8, z: 12, core: 2. Of those that a mesh axis runs over, the one named last changes fastest.
Arguments:
- climate_state: float32 [8, 768, 1024], P(None, 'face', 'tile'), may hold values from -6 to 6
- diffusive_courant: float32 [768, 1024], P('face', 'tile'), may hold values from 0.02 to 0.24
- stratum_projection: float32 [8, 8], replicated, may hold values from -2 to 2
- destination_piece: int32 [67584], P(('face', 'tile')), may hold values from 0 to 703, as said below
- shared_footprints: bfloat16 [67584, 128, 128], P(('face', 'tile')), may hold values from 0.019897461 to 0.19921875
- oceanic_departure: float32 [67584, 128], P(('face', 'tile')), may hold values from -6 to 6
- wet_indicator: int32 [67584, 128], P(('face', 'tile')), may hold values 0 or 1
- heating_response: float32 [8], replicated, may hold values from -1 to 1
Outputs:
- stepped_weather_fields: float32 [8, 768, 1024], P(None, 'face', 'tile')
- stepped_seawater_kelvin: float32 [67584, 128], P(('face', 'tile'))
- regridded_seawater_kelvin: float32 [768, 1024], P('face', 'tile')
The draws below stay inside these ranges and needn't reach their ends.
Inputs may be any that keep to these rules, and one draw needn't show every extreme that they name: destination_piece[p] // 88 is the tile index of the ocean block's owner within the pair's face group and destination_piece[p] % 88 the block on it. Within a face group every ocean block is named by exactly one pair. The 88 pairs of one device name at most 22 blocks of one tile index, and every device names exactly 22 of some tile index.
All inputs are finite; a program needn't handle non-finite values. No bound on the sum of `wet_indicator` on one device may be relied on, other than what follows from the above.
Results may differ from the reference program's by a relative error of at most 0.0018.
Values may be sent and summed in bfloat16 or wider, within the bound.
A program may use at most 32 MiB of HBM per device.

```python
import math
import jax
import jax.numpy as jnp
from jax import lax

LEV = 8
FLUX = 8
BUNDLE_CELLCOUNT = 128
SUBSTEPS = 6
FAN = 11
PARTITION_BANDS = 8
NORTHSOUTH_SIZE = 768
EASTWEST_SIZE = 1024
PAIRS_DEV = 88
OBLK_DEV = 88
NPAIR = 67584
BASIN_GROUPS = 67584
N_FACE = 96
N_TILE = 8
DEVICES = 768


def draw_destination_piece(key, part):
    key = jax.random.fold_in(key, 11)
    shift_key, order_key, local_key = jax.random.split(key, 3)
    share = PAIRS_DEV // N_TILE
    shift = jax.random.randint(shift_key, (N_FACE,), 0, N_TILE)
    tiles = jnp.arange(N_TILE, dtype=jnp.int32)
    offset = (tiles[None, None, :] - tiles[None, :, None] - shift[:, None, None]) % N_TILE
    counts = jnp.where(offset == 0, 2 * share, jnp.where(offset == 1, 0, share)).astype(jnp.int32)

    def one_row(row_counts):
        return jnp.repeat(tiles, row_counts, total_repeat_length=PAIRS_DEV)
    owners = jax.vmap(one_row)(counts.reshape(N_FACE * N_TILE, N_TILE))
    order_keys = jax.random.split(order_key, N_FACE * N_TILE)

    def shuffle(one_key, row):
        return row[jax.random.permutation(one_key, PAIRS_DEV)]
    owners = jax.vmap(shuffle)(order_keys, owners)
    grouped = owners.reshape(N_FACE, N_TILE * PAIRS_DEV)
    group_keys = jax.random.split(local_key, N_FACE)

    def one_group(group_key, row):
        order = jnp.argsort(row, stable=True)
        sorted_owner = row[order]
        position = jnp.arange(row.shape[0], dtype=jnp.int32)
        rank = position - sorted_owner * OBLK_DEV
        perms = jax.vmap(lambda inner: jax.random.permutation(inner, OBLK_DEV))(jax.random.split(group_key, N_TILE))
        coupling_coefficients = perms[sorted_owner, rank].astype(jnp.int32)
        return jnp.zeros_like(row).at[order].set(coupling_coefficients)
    locals_drawn = jax.vmap(one_group)(group_keys, grouped)
    return (grouped * OBLK_DEV + locals_drawn).reshape(-1).astype(jnp.int32)


def set_ends(entries, rng, smallest, top_value):
    longest = entries.shape.index(max(entries.shape))
    spots = []
    for shift in (0, 1):
        where = [jax.random.randint(jax.random.fold_in(rng, axis), (), 0, length) for axis, length in enumerate(entries.shape)]
        where[longest] = (where[longest] + shift) % entries.shape[longest]
        spots.append(tuple(where))
    return entries.at[spots[0]].set(smallest).at[spots[1]].set(top_value)


def levels(stream_key, dims, cuts, smallest, top_value):
    gain = 1.0
    for dim, parts in cuts:
        heights = jax.random.uniform(jax.random.fold_in(jax.random.fold_in(stream_key, 6), dim), (parts,), jnp.float32, smallest / len(cuts), top_value / len(cuts))
        gain = gain * jnp.repeat(jnp.exp(heights), dims[dim] // parts).reshape((-1,) + (1,) * (len(dims) - 1 - dim))
    return gain


def centred(rng, extent, width, bound, shards=(), kind=jnp.bfloat16):
    loudness = levels(rng, extent, shards, -0.22, 0.18) if shards else 1.0
    result = jax.random.normal(rng, extent, jnp.float32) * width * loudness
    return jnp.minimum(jnp.maximum(result, -bound), bound).astype(kind)


def setup_inputs(seed: int = 0) -> dict:
    splits = jax.random.split(jax.random.key(seed), 9)
    climate_state = centred(splits[0], (LEV, NORTHSOUTH_SIZE, EASTWEST_SIZE), 1.0, 6.0, ((1, 96), (2, 8)), jnp.float32)
    diffusive_courant = jnp.clip(jnp.exp(math.log(0.24) - 2.4849066 * jax.random.uniform(splits[1], (NORTHSOUTH_SIZE, EASTWEST_SIZE), jnp.float32) ** levels(splits[1], (NORTHSOUTH_SIZE, EASTWEST_SIZE), ((0, 96), (1, 8)), -0.2, 0.2)), 0.02, 0.24)
    stratum_projection = centred(splits[2], (FLUX, LEV), LEV ** -0.5, 2.0, (), jnp.float32)
    destination_piece = draw_destination_piece(jax.random.fold_in(splits[8], 71), 0)
    shared_footprints = jnp.clip(0.019897461 + 0.17932129 * jax.random.uniform(splits[4], (NPAIR, BUNDLE_CELLCOUNT, BUNDLE_CELLCOUNT), jnp.float32) ** levels(splits[4], (NPAIR, BUNDLE_CELLCOUNT, BUNDLE_CELLCOUNT), ((0, 768),), -0.2, 0.2), 0.019897461, 0.19921875).astype(jnp.bfloat16)
    oceanic_departure = centred(splits[5], (BASIN_GROUPS, BUNDLE_CELLCOUNT), 1.0, 6.0, ((0, 768),), jnp.float32)
    wet_indicator = set_ends((jax.random.randint(splits[6], (BASIN_GROUPS, BUNDLE_CELLCOUNT), 0, 4) < 3).astype(jnp.int32), jax.random.fold_in(splits[6], 1), 0, 1)
    heating_response = jnp.clip(jax.random.uniform(splits[7], (FLUX,), jnp.float32, -1.0, 1.0), -1.0, 1.0)
    return {"climate_state": climate_state, "diffusive_courant": diffusive_courant, "stratum_projection": stratum_projection, "destination_piece": destination_piece, "shared_footprints": shared_footprints, "oceanic_departure": oceanic_departure, "wet_indicator": wet_indicator, "heating_response": heating_response}


def reference(climate_state, diffusive_courant, stratum_projection, destination_piece, shared_footprints, oceanic_departure, wet_indicator, heating_response):
    stepped_weather_fields = climate_state
    flux = jnp.zeros((FLUX, NORTHSOUTH_SIZE, EASTWEST_SIZE), jnp.float32)
    for step in range(SUBSTEPS):
        beside_all = jnp.roll(stepped_weather_fields, -1, 1) + jnp.roll(stepped_weather_fields, 1, 1) + jnp.roll(stepped_weather_fields, -1, 2) + jnp.roll(stepped_weather_fields, 1, 2)
        stepped_weather_fields = stepped_weather_fields + diffusive_courant * (beside_all - 4.0 * stepped_weather_fields)
        flux = flux + jnp.tanh(jnp.einsum('fl,lxy->fxy', stratum_projection, stepped_weather_fields, precision=lax.Precision.HIGHEST))
    flux_low = (flux * (1.0 / SUBSTEPS)).astype(jnp.bfloat16)
    grid = flux_low.reshape(FLUX, N_FACE, PARTITION_BANDS, N_TILE, BUNDLE_CELLCOUNT).transpose(1, 3, 2, 0, 4).reshape(DEVICES, PARTITION_BANDS, FLUX, BUNDLE_CELLCOUNT)
    tiles_w = shared_footprints.reshape(DEVICES, PAIRS_DEV, BUNDLE_CELLCOUNT, BUNDLE_CELLCOUNT)
    offset = (jnp.arange(DEVICES, dtype=jnp.int32) // N_TILE) * (N_TILE * OBLK_DEV)
    global_dst = destination_piece.reshape(DEVICES, PAIRS_DEV).astype(jnp.int32) + offset[:, None]

    def remap(pieces):
        coupled_pair_ledger, tile = pieces
        source_cells = jnp.repeat(coupled_pair_ledger, FAN, axis=0).astype(jnp.float32)
        tile_flux_values = tile.astype(jnp.float32)
        colsum = jnp.sum(tile_flux_values, axis=1)
        unremapped_flux = jnp.einsum('rkd,rdy->rky', source_cells, tile_flux_values, precision=lax.Precision.HIGHEST)
        return (unremapped_flux * (1.0 / colsum)[:, None, :]).astype(jnp.bfloat16)

    partial_value = lax.map(remap, (grid, tiles_w))
    fluxes = jnp.zeros((BASIN_GROUPS, FLUX, BUNDLE_CELLCOUNT), jnp.float32).at[global_dst.reshape(-1)].add(partial_value.reshape(-1, FLUX, BUNDLE_CELLCOUNT).astype(jnp.float32))
    bottom_driving_terms = jnp.einsum('f,ofc->oc', heating_response, fluxes, precision=lax.Precision.HIGHEST)
    stepped_seawater_kelvin = oceanic_departure + wet_indicator.astype(jnp.float32) * bottom_driving_terms

    def gather_heat(pieces):
        tile, piece_ordinal_sequence = pieces
        tile_flux_values = tile.astype(jnp.float32)
        coupling_coefficients = stepped_seawater_kelvin[piece_ordinal_sequence]
        enthalpy_passage = jnp.einsum('pac,pc->pa', tile_flux_values, coupling_coefficients, precision=lax.Precision.HIGHEST)
        horizontal_totalled = jnp.sum(tile_flux_values, axis=2)
        return enthalpy_passage.reshape(PARTITION_BANDS, FAN, BUNDLE_CELLCOUNT).sum(1) / horizontal_totalled.reshape(PARTITION_BANDS, FAN, BUNDLE_CELLCOUNT).sum(1)

    enthalpy_passages = lax.map(gather_heat, (tiles_w, global_dst))
    regridded_seawater_kelvin = enthalpy_passages.reshape(N_FACE, N_TILE, PARTITION_BANDS, BUNDLE_CELLCOUNT).transpose(0, 2, 1, 3).reshape(NORTHSOUTH_SIZE, EASTWEST_SIZE)
    return stepped_weather_fields, stepped_seawater_kelvin, regridded_seawater_kelvin
```

```python
import functools

import jax
import jax.numpy as jnp
from jax import lax
from jax.experimental import pallas as pl
from jax.experimental.pallas import tpu as pltpu
from jax.sharding import PartitionSpec as P

MESH = pl.DeviceIdType.MESH
F32 = jnp.float32
BF16 = jnp.bfloat16
SUBSTEPS = 6
LEV = 8
ROWS = 8
CELLS = 128
PAIRS = 88
FAN = 11
BLOCKS = 88
TILES = 8
SLOTS = 24


def halves(x):
    hi = x.astype(BF16)
    return hi, (x - hi.astype(F32)).astype(BF16)


def select_rows(onehot, x):
    hi, lo = halves(x)
    both = jnp.dot(onehot, jnp.concatenate([hi, lo], 1), preferred_element_type=F32)
    return both[:, :CELLS] + both[:, CELLS:]


def kernel(
    faces,
    state_hbm, courant_hbm, proj_hbm, dest_hbm, w_hbm, dep_hbm, wet_hbm, heat_hbm,
    state_out, sea_out, regrid_out,
    state_v, courant_v, proj_v, dest_all, w_v, dep_v, wet_v, heat_s,
    pack, strip_first, strip_last, rows_above, rows_below, side,
    recip, den, hsum, place_t, onehot, onehot_t, place,
    sea_send, sea_recv, h_send, h_recv,
    local_sem, halo_send_sem, halo_recv_sem, peer_send_sem, peer_recv_sem,
):
    f = lax.axis_index("face")
    t = lax.axis_index("tile")
    up, down = lax.rem(f + faces - 1, faces), lax.rem(f + 1, faces)
    left, right = lax.rem(t + TILES - 1, TILES), lax.rem(t + 1, TILES)

    loads = [
        pltpu.make_async_copy(src, dst, local_sem.at[i])
        for i, (src, dst) in enumerate([
            (state_hbm, state_v), (courant_hbm, courant_v), (dest_hbm, dest_all.at[t]), (proj_hbm, proj_v),
            (heat_hbm, heat_s), (w_hbm, w_v), (dep_hbm, dep_v), (wet_hbm, wet_v),
        ])
    ]
    for load in loads:
        load.start()

    barrier = pltpu.get_barrier_semaphore()
    greet = [(fa, ti) for fa in (up, down) for ti in (left, t, right)]
    greet += [(f, lax.rem(t + k, TILES)) for k in range(1, TILES)]
    for device in greet:
        pl.semaphore_signal(barrier, inc=1, device_id=device, device_id_type=MESH)

    for k in range(3):
        side[k, 8:120, :] = jnp.zeros((112, CELLS), F32)
    for i in range(5):
        loads[i].wait()
    courant = courant_v[...]
    pack[0:8, :] = courant
    pack[72:80, :] = courant
    for r in range(ROWS):
        pack[8 + 8 * r:16 + 8 * r, :] = state_v[pl.ds(r, LEV, stride=ROWS), :]
    own = jnp.concatenate([pack[0:72, :], jnp.zeros((56, CELLS), F32)], 0)
    own_t = jnp.swapaxes(own, 0, 1)
    strip_first[...] = own_t[0:8]
    strip_last[...] = own_t[120:128]

    pl.semaphore_wait(barrier, len(greet))

    dest_copies, halo_copies = [], []
    for k in range(1, TILES):
        dest_copies.append(pltpu.make_async_remote_copy(
            src_ref=dest_all.at[t], dst_ref=dest_all.at[t], send_sem=peer_send_sem.at[k - 1], recv_sem=peer_recv_sem.at[k - 1],
            device_id=(f, lax.rem(t + k, TILES)), device_id_type=MESH))
    halo = [
        (pack.at[pl.ds(0, 56)], rows_below, (up, t)),
        (pack.at[pl.ds(24, 56)], rows_above, (down, t)),
    ]
    for face, slot in ((up, 2), (f, 1), (down, 0)):
        halo.append((strip_first, side.at[slot, pl.ds(0, 8)], (face, left)))
        halo.append((strip_last, side.at[slot, pl.ds(120, 8)], (face, right)))
    for i, (src, dst, device) in enumerate(halo):
        halo_copies.append(pltpu.make_async_remote_copy(
            src_ref=src, dst_ref=dst, send_sem=halo_send_sem.at[i], recv_sem=halo_recv_sem.at[i],
            device_id=device, device_id_type=MESH))
    for copy in dest_copies + halo_copies:
        copy.start()

    i0 = lax.broadcasted_iota(jnp.int32, (PAIRS, PAIRS), 0)
    i1 = lax.broadcasted_iota(jnp.int32, (PAIRS, PAIRS), 1)
    earlier = (i0 < i1).astype(F32).astype(BF16)
    div8 = sum((i1 >= 8 * m).astype(jnp.int32) for m in range(1, FAN))
    permute = (i0 == (i1 - 8 * div8) * FAN + div8).astype(F32).astype(BF16)
    slot_id = lax.broadcasted_iota(jnp.int32, (SLOTS, PAIRS), 0).astype(F32)
    tile_id = lax.broadcasted_iota(jnp.int32, (TILES, PAIRS), 0)

    def owner_of(dest):
        return sum((dest >= BLOCKS * m).astype(jnp.int32) for m in range(1, TILES))

    def slots_of(mask):
        wide = jnp.concatenate([mask, jnp.zeros((8, PAIRS), F32)], 0).astype(BF16)
        rank = jnp.dot(wide, earlier, preferred_element_type=F32)[:8]
        rank = jnp.where(mask > 0.5, rank, -1.0)
        return jnp.concatenate(
            [(rank[i:i + 1] == slot_id).astype(F32) for i in range(TILES)], 0)

    mine = jnp.broadcast_to(owner_of(dest_all[t]), (TILES, PAIRS))
    own_place = slots_of((mine == tile_id).astype(F32))
    placed = jnp.dot(own_place.astype(BF16), permute, preferred_element_type=F32)
    place[...] = placed.astype(BF16)
    placed = jnp.concatenate([placed, jnp.zeros((TILES * SLOTS, CELLS - PAIRS), F32)], 1)
    place_t[...] = jnp.swapaxes(placed, 0, 1)[:PAIRS].astype(BF16)

    for copy in dest_copies:
        copy.wait()
    dest = jnp.concatenate([dest_all[i] for i in range(TILES)], 0)
    owner = owner_of(dest)
    local = (dest - BLOCKS * owner + 1).astype(F32)
    asked = slots_of((owner == t).astype(F32))
    block = jnp.concatenate([
        jnp.sum(asked[SLOTS * i:SLOTS * (i + 1)] * local[i:i + 1], axis=1, keepdims=True) for i in range(TILES)], 0)
    block_id = (lax.broadcasted_iota(jnp.int32, (TILES * SLOTS, CELLS), 1) + 1).astype(F32)
    hot = (jnp.broadcast_to(block, (TILES * SLOTS, CELLS)) == block_id).astype(F32)
    onehot_t[...] = jnp.swapaxes(hot, 0, 1)[:BLOCKS].astype(BF16)
    hot = hot[:, :BLOCKS].astype(BF16)
    loads[6].wait()
    loads[7].wait()
    hi, lo = halves(dep_v[...])
    wet = wet_v[...].astype(F32)
    found = jnp.dot(hot, jnp.concatenate([hi, lo, wet.astype(BF16)], 1), preferred_element_type=F32)
    found_dep = found[:, :CELLS] + found[:, CELLS:2 * CELLS]
    found_wet = found[:, 2 * CELLS:]
    for i in range(TILES):
        sea_send[i, 0:SLOTS, :] = found_dep[SLOTS * i:SLOTS * (i + 1)]
        sea_send[i, SLOTS:2 * SLOTS, :] = found_wet[SLOTS * i:SLOTS * (i + 1)]
    sea_copies = []
    for k in range(1, TILES):
        peer = lax.rem(t + k, TILES)
        sea_copies.append(pltpu.make_async_remote_copy(
            src_ref=sea_send.at[peer], dst_ref=sea_recv.at[t],
            send_sem=peer_send_sem.at[6 + k], recv_sem=peer_recv_sem.at[6 + k],
            device_id=(f, peer), device_id_type=MESH))
        sea_copies[-1].start()
    sea_recv[t] = sea_send[t]

    loads[5].wait()
    sums = []
    for r in range(ROWS):
        total = jnp.zeros((CELLS, CELLS), F32)
        for j in range(FAN):
            w = w_v[r * FAN + j].astype(F32)
            total = total + w
            recip[8 * j + r:8 * j + r + 1, :] = jnp.sum(w, axis=0, keepdims=True)
        sums.append(jnp.sum(jnp.swapaxes(total, 0, 1), axis=0, keepdims=True))
    den[...] = jnp.concatenate(sums, 0)
    recip[...] = 1.0 / recip[...]

    proj = proj_v[...]
    levels = [jnp.broadcast_to(proj[:, l:l + 1], (LEV, CELLS)) for l in range(LEV)]
    sub = lax.broadcasted_iota(jnp.int32, (8, CELLS), 0)
    heat = jnp.zeros((8, CELLS), F32)
    for i in range(8):
        heat = jnp.where(sub == i, heat_s[i], heat)
    lane = lax.broadcasted_iota(jnp.int32, (8, CELLS), 1)
    first, last = lane == 0, lane == CELLS - 1

    for copy in halo_copies:
        copy.wait()
    sides = [jnp.swapaxes(side[k], 0, 1) for k in range(3)]
    main = [rows_above[8 * i:8 * i + 8, :] for i in range(6)]
    main += [pack[8 + 8 * r:16 + 8 * r, :] for r in range(ROWS)]
    main += [rows_below[8 + 8 * i:16 + 8 * i, :] for i in range(6)]
    outer = [sides[0][8 + 8 * r:16 + 8 * r] for r in range(2, 8)]
    outer += [sides[1][8 + 8 * r:16 + 8 * r] for r in range(8)]
    outer += [sides[2][8 + 8 * r:16 + 8 * r] for r in range(6)]
    cm = [rows_above[48 + r:49 + r, :] for r in range(2, 8)]
    cm += [courant_v[r:r + 1, :] for r in range(8)]
    cm += [rows_below[r:r + 1, :] for r in range(6)]
    co = [sides[0][r:r + 1] for r in range(2, 8)]
    co += [sides[1][r:r + 1] for r in range(8)]
    co += [sides[2][r:r + 1] for r in range(6)]

    flux = [jnp.zeros((8, CELLS), F32) for _ in range(ROWS)]
    for step in range(SUBSTEPS):
        new_main, new_outer = list(main), list(outer)
        for j in range(step + 1, 19 - step):
            m, o = main[j], outer[j]
            m_next, o_next = pltpu.roll(m, CELLS - 1, 1), pltpu.roll(o, CELLS - 1, 1)
            m_prev, o_prev = pltpu.roll(m, 1, 1), pltpu.roll(o, 1, 1)
            around = main[j + 1] + main[j - 1] + jnp.where(last, o_next, m_next) + jnp.where(first, o_prev, m_prev)
            new_main[j] = m + cm[j] * (around - 4.0 * m)
            if step < SUBSTEPS - 1:
                around = outer[j + 1] + outer[j - 1] + jnp.where(last, m_next, o_next) + jnp.where(first, m_prev, o_prev)
                new_outer[j] = o + co[j] * (around - 4.0 * o)
        main, outer = new_main, new_outer
        for r in range(ROWS):
            x = main[6 + r]
            total = levels[0] * x[0:1]
            for l in range(1, LEV):
                total = total + levels[l] * x[l:l + 1]
            flux[r] = flux[r] + jnp.tanh(total)
    for r in range(ROWS):
        state_out[pl.ds(r, LEV, stride=ROWS), :] = main[6 + r]

    weighted = []
    for r in range(ROWS):
        low = (flux[r] * (1.0 / SUBSTEPS)).astype(BF16).astype(F32)
        weighted.append(jnp.sum(low * heat, axis=0, keepdims=True))
    weighted = jnp.concatenate(weighted + [jnp.zeros((CELLS - 8, CELLS), F32)], 0)
    weighted = jnp.swapaxes(weighted, 0, 1)
    for r in range(ROWS):
        column = jnp.broadcast_to(weighted[:, r:r + 1], (CELLS, CELLS))
        for j in range(FAN):
            hsum[8 * j + r:8 * j + r + 1, :] = jnp.sum(w_v[r * FAN + j].astype(F32) * column, axis=0, keepdims=True)
    drive = hsum[...] * recip[...]
    slots = select_rows(place[...], drive)
    for i in range(TILES):
        h_send[i] = slots[SLOTS * i:SLOTS * (i + 1)]
    h_copies = []
    for k in range(1, TILES):
        peer = lax.rem(t + k, TILES)
        h_copies.append(pltpu.make_async_remote_copy(
            src_ref=h_send.at[peer], dst_ref=h_recv.at[t],
            send_sem=peer_send_sem.at[13 + k], recv_sem=peer_recv_sem.at[13 + k],
            device_id=(f, peer), device_id_type=MESH))
        h_copies[-1].start()
    h_recv[t] = h_send[t]

    for copy in sea_copies:
        copy.wait()
    got_dep = jnp.concatenate([sea_recv[i, 0:SLOTS, :] for i in range(TILES)], 0)
    got_wet = jnp.concatenate([sea_recv[i, SLOTS:2 * SLOTS, :] for i in range(TILES)], 0)
    hi, lo = halves(got_dep)
    got = jnp.dot(place_t[...], jnp.concatenate([hi, lo, got_wet.astype(BF16)], 1), preferred_element_type=F32)
    hsum[...] = got[:, :CELLS] + got[:, CELLS:2 * CELLS] + got[:, 2 * CELLS:] * drive
    sums = []
    for r in range(ROWS):
        total = jnp.zeros((CELLS, CELLS), F32)
        for j in range(FAN):
            total = total + w_v[r * FAN + j].astype(F32) * hsum[8 * j + r:8 * j + r + 1, :]
        sums.append(jnp.sum(jnp.swapaxes(total, 0, 1), axis=0, keepdims=True))
    regrid_out[...] = jnp.concatenate(sums, 0) / den[...]

    for copy in h_copies:
        copy.wait()
    got = jnp.concatenate([h_recv[i] for i in range(TILES)], 0)
    sea_out[...] = dep_v[...] + wet_v[...].astype(F32) * select_rows(onehot_t[...], got)


def body(state, courant, proj, dest, w, dep, wet, heat):
    faces = lax.axis_size("face")
    vmem = pltpu.VMEM
    hbm = pl.BlockSpec(memory_space=pltpu.HBM)
    state, sea, regrid = pl.pallas_call(
        functools.partial(kernel, faces),
        out_shape=(
            jax.ShapeDtypeStruct((LEV * ROWS, CELLS), F32),
            jax.ShapeDtypeStruct((BLOCKS, CELLS), F32),
            jax.ShapeDtypeStruct((ROWS, CELLS), F32),
        ),
        in_specs=[hbm] * 8,
        out_specs=(pl.BlockSpec(memory_space=vmem),) * 3,
        scratch_shapes=[
            vmem((LEV * ROWS, CELLS), F32), vmem((ROWS, CELLS), F32), vmem((8, 8), F32),
            vmem((TILES, 1, PAIRS), jnp.int32), vmem((PAIRS, CELLS, CELLS), BF16),
            vmem((BLOCKS, CELLS), F32), vmem((BLOCKS, CELLS), jnp.int32), pltpu.SMEM((8,), F32),
            vmem((80, CELLS), F32), vmem((8, CELLS), F32), vmem((8, CELLS), F32),
            vmem((56, CELLS), F32), vmem((56, CELLS), F32), vmem((3, CELLS, CELLS), F32),
            vmem((PAIRS, CELLS), F32), vmem((ROWS, CELLS), F32), vmem((PAIRS, CELLS), F32),
            vmem((PAIRS, TILES * SLOTS), BF16), vmem((TILES * SLOTS, BLOCKS), BF16),
            vmem((BLOCKS, TILES * SLOTS), BF16), vmem((TILES * SLOTS, PAIRS), BF16),
            vmem((TILES, 2 * SLOTS, CELLS), F32), vmem((TILES, 2 * SLOTS, CELLS), F32),
            vmem((TILES, SLOTS, CELLS), F32), vmem((TILES, SLOTS, CELLS), F32),
            pltpu.SemaphoreType.DMA((8,)), pltpu.SemaphoreType.DMA((8,)), pltpu.SemaphoreType.DMA((8,)),
            pltpu.SemaphoreType.DMA((21,)), pltpu.SemaphoreType.DMA((21,)),
        ],
        compiler_params=pltpu.CompilerParams(
            collective_id=0, has_side_effects=True, vmem_limit_bytes=32 * 1024 * 1024),
    )(state.reshape(LEV * ROWS, CELLS), courant, proj, dest.reshape(1, PAIRS), w, dep, wet, heat)
    return state.reshape(LEV, ROWS, CELLS), sea, regrid


def solution(mesh):
    both = P(("face", "tile"), None)
    return jax.shard_map(
        body,
        mesh=mesh,
        in_specs=(
            P(None, "face", "tile"), P("face", "tile"), P(), P(("face", "tile")),
            P(("face", "tile"), None, None), both, both, P(),
        ),
        out_specs=(P(None, "face", "tile"), both, P("face", "tile")),
        check_vma=False,
    )
```

```python
import functools

import jax
import jax.numpy as jnp
from jax import lax
from jax.experimental import pallas as pl
from jax.experimental.pallas import tpu as pltpu
from jax.sharding import PartitionSpec as P

MESH = pl.DeviceIdType.MESH
F32 = jnp.float32
BF16 = jnp.bfloat16
SUBSTEPS = 6
LEV = 8
ROWS = 8
CELLS = 128
PAIRS = 88
FAN = 11
BLOCKS = 88
TILES = 8
SLOTS = 24
HOT_ROWS = 96
VMEM_BYTES = 62 * 1024 * 1024


def halves(x):
    hi = x.astype(BF16)
    return hi, (x - hi.astype(F32)).astype(BF16)


def select_rows(onehot, x):
    hi, lo = halves(x)
    both = jnp.dot(onehot, jnp.concatenate([hi, lo], 1), preferred_element_type=F32)
    return both[:, :CELLS] + both[:, CELLS:]


def kernel(
    faces,
    state_hbm, courant_hbm, proj_hbm, dest_hbm, w_hbm, dep_hbm, wet_hbm, heat_hbm,
    state_out, regrid_out, hot_out, h_recv,
    state_v, courant_v, proj_v, dest_all, w_v, dep_v, wet_v, heat_s,
    pack, strip_first, strip_last, rows_above, rows_below, side,
    recip, den, hsum, place_t, onehot_t, place, stepped, regrid,
    sea_send, sea_recv, h_send,
    local_sem, halo_send_sem, halo_recv_sem, peer_send_sem, peer_recv_sem,
):
    f = lax.axis_index("face")
    t = lax.axis_index("tile")
    up, down = lax.rem(f + faces - 1, faces), lax.rem(f + 1, faces)
    left, right = lax.rem(t + TILES - 1, TILES), lax.rem(t + 1, TILES)

    barrier = pltpu.get_barrier_semaphore()
    greet = [(f, lax.rem(t + k, TILES)) for k in range(1, TILES)]
    greet += [(fa, ti) for fa in (up, down) for ti in (left, t, right)]
    for device in greet:
        pl.semaphore_signal(barrier, inc=1, device_id=device, device_id_type=MESH)

    loads = [
        pltpu.make_async_copy(src, dst, local_sem.at[i])
        for i, (src, dst) in enumerate([
            (state_hbm, state_v), (courant_hbm, courant_v), (dest_hbm, dest_all.at[t]), (proj_hbm, proj_v),
            (heat_hbm, heat_s), (w_hbm, w_v), (dep_hbm, dep_v), (wet_hbm, wet_v),
        ])
    ]
    for i in (2, 0, 1, 3, 4):
        loads[i].start()

    for k in range(3):
        side[k, 8:120, :] = jnp.zeros((112, CELLS), F32)
    pl.semaphore_wait(barrier, len(greet))
    loads[2].wait()
    dest_copies, halo_copies = [], []
    for k in range(1, TILES):
        dest_copies.append(pltpu.make_async_remote_copy(
            src_ref=dest_all.at[t], dst_ref=dest_all.at[t], send_sem=peer_send_sem.at[k - 1], recv_sem=peer_recv_sem.at[k - 1],
            device_id=(f, lax.rem(t + k, TILES)), device_id_type=MESH))
    for copy in dest_copies:
        copy.start()

    loads[0].wait()
    loads[1].wait()
    courant = courant_v[...]
    pack[0:8, :] = courant
    pack[72:80, :] = courant
    for r in range(ROWS):
        pack[8 + 8 * r:16 + 8 * r, :] = state_v[pl.ds(r, LEV, stride=ROWS), :]
    own = jnp.concatenate([pack[0:72, :], jnp.zeros((56, CELLS), F32)], 0)
    own_t = jnp.swapaxes(own, 0, 1)
    strip_first[...] = own_t[0:8]
    strip_last[...] = own_t[120:128]


    halo = [
        (pack.at[pl.ds(0, 56)], rows_below, (up, t)),
        (pack.at[pl.ds(24, 56)], rows_above, (down, t)),
    ]
    for face, slot in ((up, 2), (f, 1), (down, 0)):
        halo.append((strip_first, side.at[slot, pl.ds(0, 8)], (face, left)))
        halo.append((strip_last, side.at[slot, pl.ds(120, 8)], (face, right)))
    for i, (src, dst, device) in enumerate(halo):
        halo_copies.append(pltpu.make_async_remote_copy(
            src_ref=src, dst_ref=dst, send_sem=halo_send_sem.at[i], recv_sem=halo_recv_sem.at[i],
            device_id=device, device_id_type=MESH))
    for copy in halo_copies:
        copy.start()
    for load in loads[5:]:
        load.start()
    loads[3].wait()
    loads[4].wait()

    i0 = lax.broadcasted_iota(jnp.int32, (PAIRS, PAIRS), 0)
    i1 = lax.broadcasted_iota(jnp.int32, (PAIRS, PAIRS), 1)
    earlier = (i0 < i1).astype(F32).astype(BF16)
    div8 = sum((i1 >= 8 * m).astype(jnp.int32) for m in range(1, FAN))
    permute = (i0 == (i1 - 8 * div8) * FAN + div8).astype(F32).astype(BF16)
    slot_id = lax.broadcasted_iota(jnp.int32, (SLOTS, PAIRS), 0).astype(F32)
    tile_id = lax.broadcasted_iota(jnp.int32, (TILES, PAIRS), 0)

    def owner_of(dest):
        return sum((dest >= BLOCKS * m).astype(jnp.int32) for m in range(1, TILES))

    def slots_of(mask):
        wide = jnp.concatenate([mask, jnp.zeros((8, PAIRS), F32)], 0).astype(BF16)
        rank = jnp.dot(wide, earlier, preferred_element_type=F32)[:8]
        rank = jnp.where(mask > 0.5, rank, -1.0)
        return jnp.concatenate(
            [(rank[i:i + 1] == slot_id).astype(F32) for i in range(TILES)], 0)

    mine = jnp.broadcast_to(owner_of(dest_all[t]), (TILES, PAIRS))
    own_place = slots_of((mine == tile_id).astype(F32))
    placed = jnp.dot(own_place.astype(BF16), permute, preferred_element_type=F32)
    place[...] = placed.astype(BF16)
    placed = jnp.concatenate([placed, jnp.zeros((TILES * SLOTS, CELLS - PAIRS), F32)], 1)
    place_t[...] = jnp.swapaxes(placed, 0, 1)[:PAIRS].astype(BF16)

    loads[5].wait()
    sums = []
    for r in range(ROWS):
        total = jnp.zeros((CELLS, CELLS), F32)
        for j in range(FAN):
            w = w_v[r * FAN + j].astype(F32)
            total = total + w
            recip[8 * j + r:8 * j + r + 1, :] = jnp.sum(w, axis=0, keepdims=True)
        sums.append(jnp.sum(jnp.swapaxes(total, 0, 1), axis=0, keepdims=True))
    den[...] = jnp.concatenate(sums, 0)
    recip[...] = 1.0 / recip[...]

    for copy in dest_copies:
        copy.wait()
    dest = jnp.concatenate([dest_all[i] for i in range(TILES)], 0)
    owner = owner_of(dest)
    local = (dest - BLOCKS * owner + 1).astype(F32)
    asked = slots_of((owner == t).astype(F32))
    block = jnp.concatenate([
        jnp.sum(asked[SLOTS * i:SLOTS * (i + 1)] * local[i:i + 1], axis=1, keepdims=True) for i in range(TILES)], 0)
    block_id = (lax.broadcasted_iota(jnp.int32, (TILES * SLOTS, CELLS), 1) + 1).astype(F32)
    hot = (jnp.broadcast_to(block, (TILES * SLOTS, CELLS)) == block_id).astype(F32)
    onehot_t[...] = jnp.swapaxes(hot, 0, 1)[:HOT_ROWS].astype(BF16)
    outs = [pltpu.make_async_copy(onehot_t, hot_out, local_sem.at[9])]
    outs[0].start()
    hot = hot[:, :BLOCKS].astype(BF16)
    loads[6].wait()
    loads[7].wait()
    hi, lo = halves(dep_v[...])
    wet = wet_v[...].astype(F32)
    found = jnp.dot(hot, jnp.concatenate([hi, lo, wet.astype(BF16)], 1), preferred_element_type=F32)
    found_dep = found[:, :CELLS] + found[:, CELLS:2 * CELLS]
    found_wet = found[:, 2 * CELLS:]
    for i in range(TILES):
        sea_send[i, 0:SLOTS, :] = found_dep[SLOTS * i:SLOTS * (i + 1)]
        sea_send[i, SLOTS:2 * SLOTS, :] = found_wet[SLOTS * i:SLOTS * (i + 1)]
    sea_copies = []
    for k in range(1, TILES):
        peer = lax.rem(t + k, TILES)
        sea_copies.append(pltpu.make_async_remote_copy(
            src_ref=sea_send.at[peer], dst_ref=sea_recv.at[t],
            send_sem=peer_send_sem.at[6 + k], recv_sem=peer_recv_sem.at[6 + k],
            device_id=(f, peer), device_id_type=MESH))
        sea_copies[-1].start()
    sea_recv[t] = sea_send[t]

    proj = proj_v[...]
    levels = [jnp.broadcast_to(proj[:, l:l + 1], (LEV, CELLS)) for l in range(LEV)]
    sub = lax.broadcasted_iota(jnp.int32, (8, CELLS), 0)
    heat = jnp.zeros((8, CELLS), F32)
    for i in range(8):
        heat = jnp.where(sub == i, heat_s[i], heat)
    lane = lax.broadcasted_iota(jnp.int32, (8, CELLS), 1)
    first, last = lane == 0, lane == CELLS - 1

    for copy in halo_copies:
        copy.wait()
    sides = [jnp.swapaxes(side[k], 0, 1) for k in range(3)]
    main = [rows_above[8 * i:8 * i + 8, :] for i in range(6)]
    main += [pack[8 + 8 * r:16 + 8 * r, :] for r in range(ROWS)]
    main += [rows_below[8 + 8 * i:16 + 8 * i, :] for i in range(6)]
    outer = [sides[0][8 + 8 * r:16 + 8 * r] for r in range(2, 8)]
    outer += [sides[1][8 + 8 * r:16 + 8 * r] for r in range(8)]
    outer += [sides[2][8 + 8 * r:16 + 8 * r] for r in range(6)]
    cm = [rows_above[48 + r:49 + r, :] for r in range(2, 8)]
    cm += [courant_v[r:r + 1, :] for r in range(8)]
    cm += [rows_below[r:r + 1, :] for r in range(6)]
    co = [sides[0][r:r + 1] for r in range(2, 8)]
    co += [sides[1][r:r + 1] for r in range(8)]
    co += [sides[2][r:r + 1] for r in range(6)]

    flux = [jnp.zeros((8, CELLS), F32) for _ in range(ROWS)]
    for step in range(SUBSTEPS):
        new_main, new_outer = list(main), list(outer)
        for j in range(step + 1, 19 - step):
            m, o = main[j], outer[j]
            m_next, o_next = pltpu.roll(m, CELLS - 1, 1), pltpu.roll(o, CELLS - 1, 1)
            m_prev, o_prev = pltpu.roll(m, 1, 1), pltpu.roll(o, 1, 1)
            around = main[j + 1] + main[j - 1] + jnp.where(last, o_next, m_next) + jnp.where(first, o_prev, m_prev)
            new_main[j] = m + cm[j] * (around - 4.0 * m)
            if step < SUBSTEPS - 1:
                around = outer[j + 1] + outer[j - 1] + jnp.where(last, m_next, o_next) + jnp.where(first, m_prev, o_prev)
                new_outer[j] = o + co[j] * (around - 4.0 * o)
        main, outer = new_main, new_outer
        for r in range(ROWS):
            x = main[6 + r]
            total = levels[0] * x[0:1]
            for l in range(1, LEV):
                total = total + levels[l] * x[l:l + 1]
            flux[r] = flux[r] + jnp.tanh(total)
    for r in range(ROWS):
        stepped[pl.ds(r, LEV, stride=ROWS), :] = main[6 + r]
    outs.append(pltpu.make_async_copy(stepped, state_out, local_sem.at[8]))
    outs[1].start()

    weighted = []
    for r in range(ROWS):
        low = (flux[r] * (1.0 / SUBSTEPS)).astype(BF16).astype(F32)
        weighted.append(jnp.sum(low * heat, axis=0, keepdims=True))
    weighted = jnp.concatenate(weighted + [jnp.zeros((CELLS - 8, CELLS), F32)], 0)
    weighted = jnp.swapaxes(weighted, 0, 1)
    for r in range(ROWS):
        column = jnp.broadcast_to(weighted[:, r:r + 1], (CELLS, CELLS))
        for j in range(FAN):
            hsum[8 * j + r:8 * j + r + 1, :] = jnp.sum(w_v[r * FAN + j].astype(F32) * column, axis=0, keepdims=True)
    drive = hsum[...] * recip[...]
    slots = select_rows(place[...], drive)
    for i in range(TILES):
        h_send[i] = slots[SLOTS * i:SLOTS * (i + 1)]
    h_copies = []
    for k in range(1, TILES):
        peer = lax.rem(t + k, TILES)
        h_copies.append(pltpu.make_async_remote_copy(
            src_ref=h_send.at[peer], dst_ref=h_recv.at[t],
            send_sem=peer_send_sem.at[13 + k], recv_sem=peer_recv_sem.at[13 + k],
            device_id=(f, peer), device_id_type=MESH))
        h_copies[-1].start()
    outs.append(pltpu.make_async_copy(h_send.at[t], h_recv.at[t], local_sem.at[10]))
    outs[2].start()

    for copy in sea_copies:
        copy.wait()
    got_dep = jnp.concatenate([sea_recv[i, 0:SLOTS, :] for i in range(TILES)], 0)
    got_wet = jnp.concatenate([sea_recv[i, SLOTS:2 * SLOTS, :] for i in range(TILES)], 0)
    hi, lo = halves(got_dep)
    got = jnp.dot(place_t[...], jnp.concatenate([hi, lo, got_wet.astype(BF16)], 1), preferred_element_type=F32)
    hsum[...] = got[:, :CELLS] + got[:, CELLS:2 * CELLS] + got[:, 2 * CELLS:] * drive
    sums = []
    for r in range(ROWS):
        total = jnp.zeros((CELLS, CELLS), F32)
        for j in range(FAN):
            total = total + w_v[r * FAN + j].astype(F32) * hsum[8 * j + r:8 * j + r + 1, :]
        sums.append(jnp.sum(jnp.swapaxes(total, 0, 1), axis=0, keepdims=True))
    regrid[...] = jnp.concatenate(sums, 0) / den[...]
    outs.append(pltpu.make_async_copy(regrid, regrid_out, local_sem.at[11]))
    outs[3].start()

    for copy in outs + h_copies:
        copy.wait()


def finish(
    state_hbm, regrid_hbm, hot_hbm, drive_hbm, dep_hbm, wet_hbm,
    state_out, sea_out, regrid_out,
    state_v, regrid_v, hot_v, drive_v, dep_v, wet_v, sea_v, load_sem, store_sem,
):
    pairs = [(drive_hbm, drive_v), (hot_hbm, hot_v), (dep_hbm, dep_v), (wet_hbm, wet_v), (state_hbm, state_v), (regrid_hbm, regrid_v)]
    loads = [pltpu.make_async_copy(src, dst, load_sem.at[i]) for i, (src, dst) in enumerate(pairs)]
    for load in loads:
        load.start()
    stores = [
        pltpu.make_async_copy(src, dst, store_sem.at[i])
        for i, (src, dst) in enumerate([(state_v, state_out), (regrid_v, regrid_out), (sea_v, sea_out)])
    ]
    for load in loads[:4]:
        load.wait()
    drive = select_rows(hot_v[...], drive_v[...])[:BLOCKS]
    sea_v[...] = dep_v[...] + wet_v[...].astype(F32) * drive
    stores[2].start()
    for i in range(2):
        loads[4 + i].wait()
        stores[i].start()
    for store in stores:
        store.wait()


def body(state, courant, proj, dest, w, dep, wet, heat):
    faces = lax.axis_size("face")
    vmem = pltpu.VMEM
    anywhere = pl.BlockSpec(memory_space=pl.ANY)
    state_shape = jax.ShapeDtypeStruct((LEV * ROWS, CELLS), F32)
    sea_shape = jax.ShapeDtypeStruct((BLOCKS, CELLS), F32)
    regrid_shape = jax.ShapeDtypeStruct((ROWS, CELLS), F32)
    state, regrid, hot, drive = pl.pallas_call(
        functools.partial(kernel, faces),
        out_shape=(
            state_shape,
            regrid_shape,
            jax.ShapeDtypeStruct((HOT_ROWS, TILES * SLOTS), BF16),
            jax.ShapeDtypeStruct((TILES, SLOTS, CELLS), F32),
        ),
        in_specs=[anywhere] * 8,
        out_specs=(anywhere,) * 4,
        scratch_shapes=[
            vmem((LEV * ROWS, CELLS), F32), vmem((ROWS, CELLS), F32), vmem((8, 8), F32),
            vmem((TILES, 1, PAIRS), jnp.int32), vmem((PAIRS, CELLS, CELLS), BF16),
            vmem((BLOCKS, CELLS), F32), vmem((BLOCKS, CELLS), jnp.int32), pltpu.SMEM((8,), F32),
            vmem((80, CELLS), F32), vmem((8, CELLS), F32), vmem((8, CELLS), F32),
            vmem((56, CELLS), F32), vmem((56, CELLS), F32), vmem((3, CELLS, CELLS), F32),
            vmem((PAIRS, CELLS), F32), vmem((ROWS, CELLS), F32), vmem((PAIRS, CELLS), F32),
            vmem((PAIRS, TILES * SLOTS), BF16), vmem((HOT_ROWS, TILES * SLOTS), BF16), vmem((TILES * SLOTS, PAIRS), BF16),
            vmem((LEV * ROWS, CELLS), F32), vmem((ROWS, CELLS), F32),
            vmem((TILES, 2 * SLOTS, CELLS), F32), vmem((TILES, 2 * SLOTS, CELLS), F32), vmem((TILES, SLOTS, CELLS), F32),
            pltpu.SemaphoreType.DMA((12,)), pltpu.SemaphoreType.DMA((8,)), pltpu.SemaphoreType.DMA((8,)),
            pltpu.SemaphoreType.DMA((21,)), pltpu.SemaphoreType.DMA((21,)),
        ],
        compiler_params=pltpu.CompilerParams(collective_id=0, has_side_effects=True, vmem_limit_bytes=VMEM_BYTES),
    )(state.reshape(LEV * ROWS, CELLS), courant, proj, dest.reshape(1, PAIRS), w, dep, wet, heat)
    state, sea, regrid = pl.pallas_call(
        finish,
        out_shape=(state_shape, sea_shape, regrid_shape),
        in_specs=[anywhere] * 6,
        out_specs=(anywhere,) * 3,
        scratch_shapes=[
            vmem((LEV * ROWS, CELLS), F32), vmem((ROWS, CELLS), F32), vmem((HOT_ROWS, TILES * SLOTS), BF16),
            vmem((TILES * SLOTS, CELLS), F32), vmem((BLOCKS, CELLS), F32), vmem((BLOCKS, CELLS), jnp.int32),
            vmem((BLOCKS, CELLS), F32), pltpu.SemaphoreType.DMA((6,)), pltpu.SemaphoreType.DMA((3,)),
        ],
        compiler_params=pltpu.CompilerParams(vmem_limit_bytes=VMEM_BYTES),
    )(state, regrid, hot, drive.reshape(TILES * SLOTS, CELLS), dep, wet)
    return state.reshape(LEV, ROWS, CELLS), sea, regrid


def solution(mesh):
    both = P(("face", "tile"), None)
    return jax.shard_map(
        body,
        mesh=mesh,
        in_specs=(
            P(None, "face", "tile"), P("face", "tile"), P(), P(("face", "tile")),
            P(("face", "tile"), None, None), both, both, P(),
        ),
        out_specs=(P(None, "face", "tile"), both, P("face", "tile")),
        check_vma=False,
    )
```

```python
import functools

import jax
import jax.numpy as jnp
from jax import lax
from jax.experimental import pallas as pl
from jax.experimental.pallas import tpu as pltpu
from jax.sharding import PartitionSpec as P

MESH = pl.DeviceIdType.MESH
F32 = jnp.float32
BF16 = jnp.bfloat16
SUBSTEPS = 6
LEV = 8
ROWS = 8
CELLS = 128
PAIRS = 88
FAN = 11
BLOCKS = 88
TILES = 8
SLOTS = 24
SEA_ROWS = 80
FAR_FIRST = (5, 3, 4, 2, 6, 7, 1)
HOT_ROWS = 96
VMEM_BYTES = 62 * 1024 * 1024


def halves(x):
    hi = x.astype(BF16)
    return hi, (x - hi.astype(F32)).astype(BF16)


def select_rows(onehot, x):
    hi, lo = halves(x)
    both = jnp.dot(onehot, jnp.concatenate([hi, lo], 1), preferred_element_type=F32)
    return both[:, :CELLS] + both[:, CELLS:]


def kernel(
    faces,
    state_hbm, courant_hbm, proj_hbm, dest_hbm, w_hbm, dep_hbm, wet_hbm, heat_hbm,
    state_out, regrid_out, hot_out, h_recv,
    state_v, courant_v, proj_v, dest_all, w_v, dep_v, wet_v, heat_s,
    pack, strip_first, strip_last, rows_above, rows_below, side,
    recip, den, hsum, place_t, onehot_t, place, stepped, regrid,
    sea_send, sea_recv, h_send,
    local_sem, halo_send_sem, halo_recv_sem, peer_send_sem, peer_recv_sem,
):
    f = lax.axis_index("face")
    t = lax.axis_index("tile")
    up, down = lax.rem(f + faces - 1, faces), lax.rem(f + 1, faces)
    left, right = lax.rem(t + TILES - 1, TILES), lax.rem(t + 1, TILES)

    barrier = pltpu.get_barrier_semaphore()
    greet = [(f, lax.rem(t + k, TILES)) for k in FAR_FIRST]
    greet += [(fa, ti) for fa in (up, down) for ti in (left, t, right)]
    for device in greet:
        pl.semaphore_signal(barrier, inc=1, device_id=device, device_id_type=MESH)

    loads = [
        pltpu.make_async_copy(src, dst, local_sem.at[i])
        for i, (src, dst) in enumerate([
            (state_hbm, state_v), (courant_hbm, courant_v), (dest_hbm, dest_all.at[t]), (proj_hbm, proj_v),
            (heat_hbm, heat_s), (w_hbm, w_v), (dep_hbm, dep_v), (wet_hbm, wet_v),
        ])
    ]
    for i in (2, 0, 1, 3, 4):
        loads[i].start()

    for k in range(3):
        side[k, 8:120, :] = jnp.zeros((112, CELLS), F32)
    loads[0].wait()
    loads[1].wait()
    courant = courant_v[...]
    pack[0:8, :] = courant
    pack[72:80, :] = courant
    for r in range(ROWS):
        pack[8 + 8 * r:16 + 8 * r, :] = state_v[pl.ds(r, LEV, stride=ROWS), :]
    own = jnp.concatenate([pack[0:72, :], jnp.zeros((56, CELLS), F32)], 0)
    own_t = jnp.swapaxes(own, 0, 1)
    strip_first[...] = own_t[0:8]
    strip_last[...] = own_t[120:128]


    pl.semaphore_wait(barrier, len(greet))
    loads[2].wait()
    dest_copies, halo_copies = [], []
    for k in FAR_FIRST:
        dest_copies.append(pltpu.make_async_remote_copy(
            src_ref=dest_all.at[t], dst_ref=dest_all.at[t], send_sem=peer_send_sem.at[k - 1], recv_sem=peer_recv_sem.at[k - 1],
            device_id=(f, lax.rem(t + k, TILES)), device_id_type=MESH))
    for copy in dest_copies:
        copy.start()

    halo = [
        (pack.at[pl.ds(0, 56)], rows_below, (up, t)),
        (pack.at[pl.ds(24, 56)], rows_above, (down, t)),
    ]
    for face, slot in ((up, 2), (f, 1), (down, 0)):
        halo.append((strip_first, side.at[slot, pl.ds(0, 8)], (face, left)))
        halo.append((strip_last, side.at[slot, pl.ds(120, 8)], (face, right)))
    for i, (src, dst, device) in enumerate(halo):
        halo_copies.append(pltpu.make_async_remote_copy(
            src_ref=src, dst_ref=dst, send_sem=halo_send_sem.at[i], recv_sem=halo_recv_sem.at[i],
            device_id=device, device_id_type=MESH))
    for copy in halo_copies:
        copy.start()
    for load in loads[5:]:
        load.start()
    loads[3].wait()
    loads[4].wait()

    i0 = lax.broadcasted_iota(jnp.int32, (PAIRS, PAIRS), 0)
    i1 = lax.broadcasted_iota(jnp.int32, (PAIRS, PAIRS), 1)
    earlier = (i0 < i1).astype(F32).astype(BF16)
    div8 = sum((i1 >= 8 * m).astype(jnp.int32) for m in range(1, FAN))
    permute = (i0 == (i1 - 8 * div8) * FAN + div8).astype(F32).astype(BF16)
    slot_id = lax.broadcasted_iota(jnp.int32, (SLOTS, PAIRS), 0).astype(F32)
    tile_id = lax.broadcasted_iota(jnp.int32, (TILES, PAIRS), 0)

    def owner_of(dest):
        return sum((dest >= BLOCKS * m).astype(jnp.int32) for m in range(1, TILES))

    def slots_of(mask):
        wide = jnp.concatenate([mask, jnp.zeros((8, PAIRS), F32)], 0).astype(BF16)
        rank = jnp.dot(wide, earlier, preferred_element_type=F32)[:8]
        rank = jnp.where(mask > 0.5, rank, -1.0)
        return jnp.concatenate(
            [(rank[i:i + 1] == slot_id).astype(F32) for i in range(TILES)], 0)

    mine = jnp.broadcast_to(owner_of(dest_all[t]), (TILES, PAIRS))
    own_place = slots_of((mine == tile_id).astype(F32))
    placed = jnp.dot(own_place.astype(BF16), permute, preferred_element_type=F32)
    place[...] = placed.astype(BF16)
    placed = jnp.concatenate([placed, jnp.zeros((TILES * SLOTS, CELLS - PAIRS), F32)], 1)
    place_t[...] = jnp.swapaxes(placed, 0, 1)[:PAIRS].astype(BF16)

    loads[5].wait()
    sums = []
    for r in range(ROWS):
        total = jnp.zeros((CELLS, CELLS), F32)
        for j in range(FAN):
            w = w_v[r * FAN + j].astype(F32)
            total = total + w
            recip[8 * j + r:8 * j + r + 1, :] = jnp.sum(w, axis=0, keepdims=True)
        sums.append(jnp.sum(jnp.swapaxes(total, 0, 1), axis=0, keepdims=True))
    den[...] = jnp.concatenate(sums, 0)
    recip[...] = 1.0 / recip[...]

    loads[6].wait()
    loads[7].wait()
    hi, lo = halves(dep_v[...])
    blocks = jnp.concatenate([hi, lo, wet_v[...].astype(F32).astype(BF16)], 1)
    block_id = (lax.broadcasted_iota(jnp.int32, (TILES * SLOTS, CELLS), 1) + 1).astype(F32)
    for copy in dest_copies:
        copy.wait()
    local = jnp.concatenate([dest_all[i] for i in range(TILES)], 0) - BLOCKS * t
    asked = slots_of(((local >= 0) & (local < BLOCKS)).astype(F32))
    local = (local + 1).astype(F32)
    block = jnp.concatenate([
        jnp.sum(asked[SLOTS * i:SLOTS * (i + 1)] * local[i:i + 1], axis=1, keepdims=True) for i in range(TILES)], 0)
    hot = (jnp.broadcast_to(block, (TILES * SLOTS, CELLS)) == block_id).astype(F32)
    found = jnp.dot(hot[:, :BLOCKS].astype(BF16), blocks, preferred_element_type=F32)
    for i in range(TILES):
        rows = found[SLOTS * i:SLOTS * (i + 1)]
        rows = [rows[:, CELLS * part:CELLS * (part + 1)] for part in range(3)]
        sea_send[i] = jnp.concatenate(rows + [jnp.zeros((SEA_ROWS - 3 * SLOTS, CELLS), F32)], 0).astype(BF16)
    sea_copies = []
    for k in FAR_FIRST:
        peer = lax.rem(t + k, TILES)
        sea_copies.append(pltpu.make_async_remote_copy(
            src_ref=sea_send.at[peer], dst_ref=sea_recv.at[t],
            send_sem=peer_send_sem.at[6 + k], recv_sem=peer_recv_sem.at[6 + k],
            device_id=(f, peer), device_id_type=MESH))
        sea_copies[-1].start()
    sea_recv[t] = sea_send[t]
    onehot_t[...] = jnp.swapaxes(hot, 0, 1)[:HOT_ROWS].astype(BF16)
    outs = [pltpu.make_async_copy(onehot_t, hot_out, local_sem.at[9])]
    outs[0].start()

    proj = proj_v[...]
    levels = [jnp.broadcast_to(proj[:, l:l + 1], (LEV, CELLS)) for l in range(LEV)]
    sub = lax.broadcasted_iota(jnp.int32, (8, CELLS), 0)
    heat = jnp.zeros((8, CELLS), F32)
    for i in range(8):
        heat = jnp.where(sub == i, heat_s[i], heat)
    lane = lax.broadcasted_iota(jnp.int32, (8, CELLS), 1)
    first, last = lane == 0, lane == CELLS - 1

    for copy in halo_copies:
        copy.wait()
    sides = [jnp.swapaxes(side[k], 0, 1) for k in range(3)]
    main = [rows_above[8 * i:8 * i + 8, :] for i in range(6)]
    main += [pack[8 + 8 * r:16 + 8 * r, :] for r in range(ROWS)]
    main += [rows_below[8 + 8 * i:16 + 8 * i, :] for i in range(6)]
    outer = [sides[0][8 + 8 * r:16 + 8 * r] for r in range(2, 8)]
    outer += [sides[1][8 + 8 * r:16 + 8 * r] for r in range(8)]
    outer += [sides[2][8 + 8 * r:16 + 8 * r] for r in range(6)]
    cm = [rows_above[48 + r:49 + r, :] for r in range(2, 8)]
    cm += [courant_v[r:r + 1, :] for r in range(8)]
    cm += [rows_below[r:r + 1, :] for r in range(6)]
    co = [sides[0][r:r + 1] for r in range(2, 8)]
    co += [sides[1][r:r + 1] for r in range(8)]
    co += [sides[2][r:r + 1] for r in range(6)]

    flux = [jnp.zeros((8, CELLS), F32) for _ in range(ROWS)]
    for step in range(SUBSTEPS):
        new_main, new_outer = list(main), list(outer)
        for j in range(step + 1, 19 - step):
            m, o = main[j], outer[j]
            m_next, o_next = pltpu.roll(m, CELLS - 1, 1), pltpu.roll(o, CELLS - 1, 1)
            m_prev, o_prev = pltpu.roll(m, 1, 1), pltpu.roll(o, 1, 1)
            around = main[j + 1] + main[j - 1] + jnp.where(last, o_next, m_next) + jnp.where(first, o_prev, m_prev)
            new_main[j] = m + cm[j] * (around - 4.0 * m)
            if step < SUBSTEPS - 1:
                around = outer[j + 1] + outer[j - 1] + jnp.where(last, m_next, o_next) + jnp.where(first, m_prev, o_prev)
                new_outer[j] = o + co[j] * (around - 4.0 * o)
        main, outer = new_main, new_outer
        for r in range(ROWS):
            x = main[6 + r]
            total = levels[0] * x[0:1]
            for l in range(1, LEV):
                total = total + levels[l] * x[l:l + 1]
            flux[r] = flux[r] + jnp.tanh(total)
    for r in range(ROWS):
        stepped[pl.ds(r, LEV, stride=ROWS), :] = main[6 + r]
    outs.append(pltpu.make_async_copy(stepped, state_out, local_sem.at[8]))
    outs[1].start()

    weighted = []
    for r in range(ROWS):
        low = (flux[r] * (1.0 / SUBSTEPS)).astype(BF16).astype(F32)
        weighted.append(jnp.sum(low * heat, axis=0, keepdims=True))
    weighted = jnp.concatenate(weighted + [jnp.zeros((CELLS - 8, CELLS), F32)], 0)
    weighted = jnp.swapaxes(weighted, 0, 1)
    for r in range(ROWS):
        column = jnp.broadcast_to(weighted[:, r:r + 1], (CELLS, CELLS))
        for j in range(FAN):
            hsum[8 * j + r:8 * j + r + 1, :] = jnp.sum(w_v[r * FAN + j].astype(F32) * column, axis=0, keepdims=True)
    drive = hsum[...] * recip[...]
    slots = select_rows(place[...], drive)
    for i in range(TILES):
        h_send[i] = slots[SLOTS * i:SLOTS * (i + 1)]
    h_copies = []
    for k in FAR_FIRST:
        peer = lax.rem(t + k, TILES)
        h_copies.append(pltpu.make_async_remote_copy(
            src_ref=h_send.at[peer], dst_ref=h_recv.at[t],
            send_sem=peer_send_sem.at[13 + k], recv_sem=peer_recv_sem.at[13 + k],
            device_id=(f, peer), device_id_type=MESH))
        h_copies[-1].start()
    outs.append(pltpu.make_async_copy(h_send.at[t], h_recv.at[t], local_sem.at[10]))
    outs[2].start()

    for copy in sea_copies:
        copy.wait()
    pieces = [sea_recv[i].astype(F32) for i in range(TILES)]
    parts = [jnp.concatenate([p[SLOTS * part:SLOTS * (part + 1)] for p in pieces], 0) for part in range(3)]
    got = jnp.dot(place_t[...], jnp.concatenate(parts, 1).astype(BF16), preferred_element_type=F32)
    hsum[...] = got[:, :CELLS] + got[:, CELLS:2 * CELLS] + got[:, 2 * CELLS:] * drive
    sums = []
    for r in range(ROWS):
        total = jnp.zeros((CELLS, CELLS), F32)
        for j in range(FAN):
            total = total + w_v[r * FAN + j].astype(F32) * hsum[8 * j + r:8 * j + r + 1, :]
        sums.append(jnp.sum(jnp.swapaxes(total, 0, 1), axis=0, keepdims=True))
    regrid[...] = jnp.concatenate(sums, 0) / den[...]
    outs.append(pltpu.make_async_copy(regrid, regrid_out, local_sem.at[11]))
    outs[3].start()

    for copy in outs + h_copies:
        copy.wait()


def finish(
    state_hbm, regrid_hbm, hot_hbm, drive_hbm, dep_hbm, wet_hbm,
    state_out, sea_out, regrid_out,
    state_v, regrid_v, hot_v, drive_v, dep_v, wet_v, sea_v, load_sem, store_sem,
):
    pairs = [(drive_hbm, drive_v), (hot_hbm, hot_v), (dep_hbm, dep_v), (wet_hbm, wet_v), (state_hbm, state_v), (regrid_hbm, regrid_v)]
    loads = [pltpu.make_async_copy(src, dst, load_sem.at[i]) for i, (src, dst) in enumerate(pairs)]
    for load in loads:
        load.start()
    stores = [
        pltpu.make_async_copy(src, dst, store_sem.at[i])
        for i, (src, dst) in enumerate([(state_v, state_out), (regrid_v, regrid_out), (sea_v, sea_out)])
    ]
    for load in loads[:4]:
        load.wait()
    drive = select_rows(hot_v[...], drive_v[...])[:BLOCKS]
    sea_v[...] = dep_v[...] + wet_v[...].astype(F32) * drive
    stores[2].start()
    for i in range(2):
        loads[4 + i].wait()
        stores[i].start()
    for store in stores:
        store.wait()


def body(state, courant, proj, dest, w, dep, wet, heat):
    faces = lax.axis_size("face")
    vmem = pltpu.VMEM
    anywhere = pl.BlockSpec(memory_space=pl.ANY)
    state_shape = jax.ShapeDtypeStruct((LEV * ROWS, CELLS), F32)
    sea_shape = jax.ShapeDtypeStruct((BLOCKS, CELLS), F32)
    regrid_shape = jax.ShapeDtypeStruct((ROWS, CELLS), F32)
    state, regrid, hot, drive = pl.pallas_call(
        functools.partial(kernel, faces),
        out_shape=(
            state_shape,
            regrid_shape,
            jax.ShapeDtypeStruct((HOT_ROWS, TILES * SLOTS), BF16),
            jax.ShapeDtypeStruct((TILES, SLOTS, CELLS), F32),
        ),
        in_specs=[anywhere] * 8,
        out_specs=(anywhere,) * 4,
        scratch_shapes=[
            vmem((LEV * ROWS, CELLS), F32), vmem((ROWS, CELLS), F32), vmem((8, 8), F32),
            vmem((TILES, 1, PAIRS), jnp.int32), vmem((PAIRS, CELLS, CELLS), BF16),
            vmem((BLOCKS, CELLS), F32), vmem((BLOCKS, CELLS), jnp.int32), pltpu.SMEM((8,), F32),
            vmem((80, CELLS), F32), vmem((8, CELLS), F32), vmem((8, CELLS), F32),
            vmem((56, CELLS), F32), vmem((56, CELLS), F32), vmem((3, CELLS, CELLS), F32),
            vmem((PAIRS, CELLS), F32), vmem((ROWS, CELLS), F32), vmem((PAIRS, CELLS), F32),
            vmem((PAIRS, TILES * SLOTS), BF16), vmem((HOT_ROWS, TILES * SLOTS), BF16), vmem((TILES * SLOTS, PAIRS), BF16),
            vmem((LEV * ROWS, CELLS), F32), vmem((ROWS, CELLS), F32),
            vmem((TILES, SEA_ROWS, CELLS), BF16), vmem((TILES, SEA_ROWS, CELLS), BF16), vmem((TILES, SLOTS, CELLS), F32),
            pltpu.SemaphoreType.DMA((12,)), pltpu.SemaphoreType.DMA((8,)), pltpu.SemaphoreType.DMA((8,)),
            pltpu.SemaphoreType.DMA((21,)), pltpu.SemaphoreType.DMA((21,)),
        ],
        compiler_params=pltpu.CompilerParams(collective_id=0, has_side_effects=True, vmem_limit_bytes=VMEM_BYTES),
    )(state.reshape(LEV * ROWS, CELLS), courant, proj, dest.reshape(1, PAIRS), w, dep, wet, heat)
    state, sea, regrid = pl.pallas_call(
        finish,
        out_shape=(state_shape, sea_shape, regrid_shape),
        in_specs=[anywhere] * 6,
        out_specs=(anywhere,) * 3,
        scratch_shapes=[
            vmem((LEV * ROWS, CELLS), F32), vmem((ROWS, CELLS), F32), vmem((HOT_ROWS, TILES * SLOTS), BF16),
            vmem((TILES * SLOTS, CELLS), F32), vmem((BLOCKS, CELLS), F32), vmem((BLOCKS, CELLS), jnp.int32),
            vmem((BLOCKS, CELLS), F32), pltpu.SemaphoreType.DMA((6,)), pltpu.SemaphoreType.DMA((3,)),
        ],
        compiler_params=pltpu.CompilerParams(vmem_limit_bytes=VMEM_BYTES),
    )(state, regrid, hot, drive.reshape(TILES * SLOTS, CELLS), dep, wet)
    return state.reshape(LEV, ROWS, CELLS), sea, regrid


def solution(mesh):
    both = P(("face", "tile"), None)
    return jax.shard_map(
        body,
        mesh=mesh,
        in_specs=(
            P(None, "face", "tile"), P("face", "tile"), P(), P(("face", "tile")),
            P(("face", "tile"), None, None), both, both, P(),
        ),
        out_specs=(P(None, "face", "tile"), both, P("face", "tile")),
        check_vma=False,
    )
```

```python
import functools

import jax
import jax.numpy as jnp
from jax import lax
from jax.experimental import pallas as pl
from jax.experimental.pallas import tpu as pltpu
from jax.sharding import PartitionSpec as P

MESH = pl.DeviceIdType.MESH
F32 = jnp.float32
BF16 = jnp.bfloat16
SUBSTEPS = 6
LEV = 8
ROWS = 8
CELLS = 128
PAIRS = 88
FAN = 11
BLOCKS = 88
TILES = 8
SLOTS = 24
SEA_ROWS = 80
FAR_FIRST = (5, 3, 4, 2, 6, 7, 1)
HOT_ROWS = 96
VMEM_BYTES = 62 * 1024 * 1024


def halves(x):
    hi = x.astype(BF16)
    return hi, (x - hi.astype(F32)).astype(BF16)


def select_rows(onehot, x):
    hi, lo = halves(x)
    both = jnp.dot(onehot, jnp.concatenate([hi, lo], 1), preferred_element_type=F32)
    return both[:, :CELLS] + both[:, CELLS:]


def kernel(
    faces,
    state_hbm, courant_hbm, proj_hbm, dest_hbm, w_hbm, dep_hbm, wet_hbm, heat_hbm,
    state_out, regrid_out, hot_out, h_recv,
    state_v, courant_v, proj_v, dest_all, w_v, dep_v, wet_v, heat_s,
    pack, strip_first, strip_last, rows_above, rows_below, side,
    recip, den, hsum, place_t, onehot_t, place, stepped, regrid,
    sea_send, sea_recv, h_send,
    local_sem, halo_send_sem, halo_recv_sem, peer_send_sem, peer_recv_sem,
):
    f = lax.axis_index("face")
    t = lax.axis_index("tile")
    up, down = lax.rem(f + faces - 1, faces), lax.rem(f + 1, faces)
    left, right = lax.rem(t + TILES - 1, TILES), lax.rem(t + 1, TILES)

    barrier = pltpu.get_barrier_semaphore()
    greet = [(f, lax.rem(t + k, TILES)) for k in FAR_FIRST]
    greet += [(fa, ti) for ti in (left, right, t) for fa in (up, down)]
    for device in greet:
        pl.semaphore_signal(barrier, inc=1, device_id=device, device_id_type=MESH)

    loads = [
        pltpu.make_async_copy(src, dst, local_sem.at[i])
        for i, (src, dst) in enumerate([
            (state_hbm, state_v), (courant_hbm, courant_v), (dest_hbm, dest_all.at[t]), (proj_hbm, proj_v),
            (heat_hbm, heat_s), (w_hbm, w_v), (dep_hbm, dep_v), (wet_hbm, wet_v),
        ])
    ]
    for i in (2, 0, 1, 3, 4):
        loads[i].start()

    for k in range(3):
        side[k, 8:120, :] = jnp.zeros((112, CELLS), F32)
    loads[0].wait()
    loads[1].wait()
    courant = courant_v[...]
    pack[0:8, :] = courant
    pack[72:80, :] = courant
    for r in range(ROWS):
        pack[8 + 8 * r:16 + 8 * r, :] = state_v[pl.ds(r, LEV, stride=ROWS), :]
    own = jnp.concatenate([pack[0:72, :], jnp.zeros((56, CELLS), F32)], 0)
    own_t = jnp.swapaxes(own, 0, 1)
    strip_first[...] = own_t[0:8]
    strip_last[...] = own_t[120:128]


    pl.semaphore_wait(barrier, len(greet))
    loads[2].wait()
    dest_copies, halo_copies = [], []
    for k in FAR_FIRST:
        dest_copies.append(pltpu.make_async_remote_copy(
            src_ref=dest_all.at[t], dst_ref=dest_all.at[t], send_sem=peer_send_sem.at[k - 1], recv_sem=peer_recv_sem.at[k - 1],
            device_id=(f, lax.rem(t + k, TILES)), device_id_type=MESH))
    for copy in dest_copies:
        copy.start()

    halo = []
    for face, slot in ((up, 2), (down, 0), (f, 1)):
        halo.append((strip_first, side.at[slot, pl.ds(0, 8)], (face, left)))
        halo.append((strip_last, side.at[slot, pl.ds(120, 8)], (face, right)))
    halo.append((pack.at[pl.ds(0, 56)], rows_below, (up, t)))
    halo.append((pack.at[pl.ds(24, 56)], rows_above, (down, t)))
    for i, (src, dst, device) in enumerate(halo):
        halo_copies.append(pltpu.make_async_remote_copy(
            src_ref=src, dst_ref=dst, send_sem=halo_send_sem.at[i], recv_sem=halo_recv_sem.at[i],
            device_id=device, device_id_type=MESH))
    for copy in halo_copies:
        copy.start()
    for load in loads[5:]:
        load.start()
    loads[3].wait()
    loads[4].wait()

    i0 = lax.broadcasted_iota(jnp.int32, (PAIRS, PAIRS), 0)
    i1 = lax.broadcasted_iota(jnp.int32, (PAIRS, PAIRS), 1)
    earlier = (i0 < i1).astype(F32).astype(BF16)
    div8 = sum((i1 >= 8 * m).astype(jnp.int32) for m in range(1, FAN))
    permute = (i0 == (i1 - 8 * div8) * FAN + div8).astype(F32).astype(BF16)
    slot_id = lax.broadcasted_iota(jnp.int32, (SLOTS, PAIRS), 0).astype(F32)
    tile_id = lax.broadcasted_iota(jnp.int32, (TILES, PAIRS), 0)

    def owner_of(dest):
        return sum((dest >= BLOCKS * m).astype(jnp.int32) for m in range(1, TILES))

    def slots_of(mask):
        wide = jnp.concatenate([mask, jnp.zeros((8, PAIRS), F32)], 0).astype(BF16)
        rank = jnp.dot(wide, earlier, preferred_element_type=F32)[:8]
        rank = jnp.where(mask > 0.5, rank, -1.0)
        return jnp.concatenate(
            [(rank[i:i + 1] == slot_id).astype(F32) for i in range(TILES)], 0)

    mine = jnp.broadcast_to(owner_of(dest_all[t]), (TILES, PAIRS))
    own_place = slots_of((mine == tile_id).astype(F32))
    placed = jnp.dot(own_place.astype(BF16), permute, preferred_element_type=F32)
    place[...] = placed.astype(BF16)
    placed = jnp.concatenate([placed, jnp.zeros((TILES * SLOTS, CELLS - PAIRS), F32)], 1)
    place_t[...] = jnp.swapaxes(placed, 0, 1)[:PAIRS].astype(BF16)

    loads[5].wait()
    sums = []
    for r in range(ROWS):
        total = jnp.zeros((CELLS, CELLS), F32)
        for j in range(FAN):
            w = w_v[r * FAN + j].astype(F32)
            total = total + w
            recip[8 * j + r:8 * j + r + 1, :] = jnp.sum(w, axis=0, keepdims=True)
        sums.append(jnp.sum(jnp.swapaxes(total, 0, 1), axis=0, keepdims=True))
    den[...] = jnp.concatenate(sums, 0)
    recip[...] = 1.0 / recip[...]

    loads[6].wait()
    loads[7].wait()
    hi, lo = halves(dep_v[...])
    blocks = jnp.concatenate([hi, lo, wet_v[...].astype(F32).astype(BF16)], 1)
    block_id = (lax.broadcasted_iota(jnp.int32, (TILES * SLOTS, CELLS), 1) + 1).astype(F32)
    for copy in dest_copies:
        copy.wait_recv()
    local = jnp.concatenate([dest_all[i] for i in range(TILES)], 0) - BLOCKS * t
    asked = slots_of(((local >= 0) & (local < BLOCKS)).astype(F32))
    local = (local + 1).astype(F32)
    block = jnp.concatenate([
        jnp.sum(asked[SLOTS * i:SLOTS * (i + 1)] * local[i:i + 1], axis=1, keepdims=True) for i in range(TILES)], 0)
    hot = (jnp.broadcast_to(block, (TILES * SLOTS, CELLS)) == block_id).astype(F32)
    found = jnp.dot(hot[:, :BLOCKS].astype(BF16), blocks, preferred_element_type=F32)
    for i in range(TILES):
        rows = found[SLOTS * i:SLOTS * (i + 1)]
        rows = [rows[:, CELLS * part:CELLS * (part + 1)] for part in range(3)]
        sea_send[i] = jnp.concatenate(rows + [jnp.zeros((SEA_ROWS - 3 * SLOTS, CELLS), F32)], 0).astype(BF16)
    sea_copies = []
    for k in FAR_FIRST:
        peer = lax.rem(t + k, TILES)
        sea_copies.append(pltpu.make_async_remote_copy(
            src_ref=sea_send.at[peer], dst_ref=sea_recv.at[t],
            send_sem=peer_send_sem.at[6 + k], recv_sem=peer_recv_sem.at[6 + k],
            device_id=(f, peer), device_id_type=MESH))
        sea_copies[-1].start()
    sea_recv[t] = sea_send[t]
    onehot_t[...] = jnp.swapaxes(hot, 0, 1)[:HOT_ROWS].astype(BF16)
    outs = [pltpu.make_async_copy(onehot_t, hot_out, local_sem.at[9])]
    outs[0].start()

    proj = proj_v[...]
    levels = [jnp.broadcast_to(proj[:, l:l + 1], (LEV, CELLS)) for l in range(LEV)]
    sub = lax.broadcasted_iota(jnp.int32, (8, CELLS), 0)
    heat = jnp.zeros((8, CELLS), F32)
    for i in range(8):
        heat = jnp.where(sub == i, heat_s[i], heat)
    lane = lax.broadcasted_iota(jnp.int32, (8, CELLS), 1)
    first, last = lane == 0, lane == CELLS - 1

    for copy in halo_copies:
        copy.wait_recv()
    sides = [jnp.swapaxes(side[k], 0, 1) for k in range(3)]
    main = [rows_above[8 * i:8 * i + 8, :] for i in range(6)]
    main += [pack[8 + 8 * r:16 + 8 * r, :] for r in range(ROWS)]
    main += [rows_below[8 + 8 * i:16 + 8 * i, :] for i in range(6)]
    outer = [sides[0][8 + 8 * r:16 + 8 * r] for r in range(2, 8)]
    outer += [sides[1][8 + 8 * r:16 + 8 * r] for r in range(8)]
    outer += [sides[2][8 + 8 * r:16 + 8 * r] for r in range(6)]
    cm = [rows_above[48 + r:49 + r, :] for r in range(2, 8)]
    cm += [courant_v[r:r + 1, :] for r in range(8)]
    cm += [rows_below[r:r + 1, :] for r in range(6)]
    co = [sides[0][r:r + 1] for r in range(2, 8)]
    co += [sides[1][r:r + 1] for r in range(8)]
    co += [sides[2][r:r + 1] for r in range(6)]

    flux = [jnp.zeros((8, CELLS), F32) for _ in range(ROWS)]
    for step in range(SUBSTEPS):
        new_main, new_outer = list(main), list(outer)
        for j in range(step + 1, 19 - step):
            m, o = main[j], outer[j]
            m_next, o_next = pltpu.roll(m, CELLS - 1, 1), pltpu.roll(o, CELLS - 1, 1)
            m_prev, o_prev = pltpu.roll(m, 1, 1), pltpu.roll(o, 1, 1)
            around = main[j + 1] + main[j - 1] + jnp.where(last, o_next, m_next) + jnp.where(first, o_prev, m_prev)
            new_main[j] = m + cm[j] * (around - 4.0 * m)
            if step < SUBSTEPS - 1:
                around = outer[j + 1] + outer[j - 1] + jnp.where(last, m_next, o_next) + jnp.where(first, m_prev, o_prev)
                new_outer[j] = o + co[j] * (around - 4.0 * o)
        main, outer = new_main, new_outer
        for r in range(ROWS):
            x = main[6 + r]
            total = levels[0] * x[0:1]
            for l in range(1, LEV):
                total = total + levels[l] * x[l:l + 1]
            flux[r] = flux[r] + jnp.tanh(total)
    for r in range(ROWS):
        stepped[pl.ds(r, LEV, stride=ROWS), :] = main[6 + r]
    outs.append(pltpu.make_async_copy(stepped, state_out, local_sem.at[8]))
    outs[1].start()

    weighted = []
    for r in range(ROWS):
        low = (flux[r] * (1.0 / SUBSTEPS)).astype(BF16).astype(F32)
        weighted.append(jnp.sum(low * heat, axis=0, keepdims=True))
    weighted = jnp.concatenate(weighted + [jnp.zeros((CELLS - 8, CELLS), F32)], 0)
    weighted = jnp.swapaxes(weighted, 0, 1)
    for r in range(ROWS):
        column = jnp.broadcast_to(weighted[:, r:r + 1], (CELLS, CELLS))
        for j in range(FAN):
            hsum[8 * j + r:8 * j + r + 1, :] = jnp.sum(w_v[r * FAN + j].astype(F32) * column, axis=0, keepdims=True)
    drive = hsum[...] * recip[...]
    slots = select_rows(place[...], drive)
    for i in range(TILES):
        h_send[i] = slots[SLOTS * i:SLOTS * (i + 1)]
    h_copies = []
    for k in FAR_FIRST:
        peer = lax.rem(t + k, TILES)
        h_copies.append(pltpu.make_async_remote_copy(
            src_ref=h_send.at[peer], dst_ref=h_recv.at[t],
            send_sem=peer_send_sem.at[13 + k], recv_sem=peer_recv_sem.at[13 + k],
            device_id=(f, peer), device_id_type=MESH))
        h_copies[-1].start()
    outs.append(pltpu.make_async_copy(h_send.at[t], h_recv.at[t], local_sem.at[10]))
    outs[2].start()

    for copy in sea_copies:
        copy.wait_recv()
    pieces = [sea_recv[i].astype(F32) for i in range(TILES)]
    parts = [jnp.concatenate([p[SLOTS * part:SLOTS * (part + 1)] for p in pieces], 0) for part in range(3)]
    got = jnp.dot(place_t[...], jnp.concatenate(parts, 1).astype(BF16), preferred_element_type=F32)
    hsum[...] = got[:, :CELLS] + got[:, CELLS:2 * CELLS] + got[:, 2 * CELLS:] * drive
    sums = []
    for r in range(ROWS):
        total = jnp.zeros((CELLS, CELLS), F32)
        for j in range(FAN):
            total = total + w_v[r * FAN + j].astype(F32) * hsum[8 * j + r:8 * j + r + 1, :]
        sums.append(jnp.sum(jnp.swapaxes(total, 0, 1), axis=0, keepdims=True))
    regrid[...] = jnp.concatenate(sums, 0) / den[...]
    outs.append(pltpu.make_async_copy(regrid, regrid_out, local_sem.at[11]))
    outs[3].start()

    for copy in outs + h_copies:
        copy.wait()
    for copy in dest_copies + halo_copies + sea_copies:
        copy.wait_send()


def finish(
    state_hbm, regrid_hbm, hot_hbm, drive_hbm, dep_hbm, wet_hbm,
    state_out, sea_out, regrid_out,
    state_v, regrid_v, hot_v, drive_v, dep_v, wet_v, sea_v, load_sem, store_sem,
):
    pairs = [(drive_hbm, drive_v), (hot_hbm, hot_v), (dep_hbm, dep_v), (wet_hbm, wet_v), (state_hbm, state_v), (regrid_hbm, regrid_v)]
    loads = [pltpu.make_async_copy(src, dst, load_sem.at[i]) for i, (src, dst) in enumerate(pairs)]
    for load in loads:
        load.start()
    stores = [
        pltpu.make_async_copy(src, dst, store_sem.at[i])
        for i, (src, dst) in enumerate([(state_v, state_out), (regrid_v, regrid_out), (sea_v, sea_out)])
    ]
    for load in loads[:4]:
        load.wait()
    drive = select_rows(hot_v[...], drive_v[...])[:BLOCKS]
    sea_v[...] = dep_v[...] + wet_v[...].astype(F32) * drive
    stores[2].start()
    for i in range(2):
        loads[4 + i].wait()
        stores[i].start()
    for store in stores:
        store.wait()


def body(state, courant, proj, dest, w, dep, wet, heat):
    faces = lax.axis_size("face")
    vmem = pltpu.VMEM
    anywhere = pl.BlockSpec(memory_space=pl.ANY)
    state_shape = jax.ShapeDtypeStruct((LEV * ROWS, CELLS), F32)
    sea_shape = jax.ShapeDtypeStruct((BLOCKS, CELLS), F32)
    regrid_shape = jax.ShapeDtypeStruct((ROWS, CELLS), F32)
    state, regrid, hot, drive = pl.pallas_call(
        functools.partial(kernel, faces),
        out_shape=(
            state_shape,
            regrid_shape,
            jax.ShapeDtypeStruct((HOT_ROWS, TILES * SLOTS), BF16),
            jax.ShapeDtypeStruct((TILES, SLOTS, CELLS), F32),
        ),
        in_specs=[anywhere] * 8,
        out_specs=(anywhere,) * 4,
        scratch_shapes=[
            vmem((LEV * ROWS, CELLS), F32), vmem((ROWS, CELLS), F32), vmem((8, 8), F32),
            vmem((TILES, 1, PAIRS), jnp.int32), vmem((PAIRS, CELLS, CELLS), BF16),
            vmem((BLOCKS, CELLS), F32), vmem((BLOCKS, CELLS), jnp.int32), pltpu.SMEM((8,), F32),
            vmem((80, CELLS), F32), vmem((8, CELLS), F32), vmem((8, CELLS), F32),
            vmem((56, CELLS), F32), vmem((56, CELLS), F32), vmem((3, CELLS, CELLS), F32),
            vmem((PAIRS, CELLS), F32), vmem((ROWS, CELLS), F32), vmem((PAIRS, CELLS), F32),
            vmem((PAIRS, TILES * SLOTS), BF16), vmem((HOT_ROWS, TILES * SLOTS), BF16), vmem((TILES * SLOTS, PAIRS), BF16),
            vmem((LEV * ROWS, CELLS), F32), vmem((ROWS, CELLS), F32),
            vmem((TILES, SEA_ROWS, CELLS), BF16), vmem((TILES, SEA_ROWS, CELLS), BF16), vmem((TILES, SLOTS, CELLS), F32),
            pltpu.SemaphoreType.DMA((12,)), pltpu.SemaphoreType.DMA((8,)), pltpu.SemaphoreType.DMA((8,)),
            pltpu.SemaphoreType.DMA((21,)), pltpu.SemaphoreType.DMA((21,)),
        ],
        compiler_params=pltpu.CompilerParams(collective_id=0, has_side_effects=True, vmem_limit_bytes=VMEM_BYTES),
    )(state.reshape(LEV * ROWS, CELLS), courant, proj, dest.reshape(1, PAIRS), w, dep, wet, heat)
    state, sea, regrid = pl.pallas_call(
        finish,
        out_shape=(state_shape, sea_shape, regrid_shape),
        in_specs=[anywhere] * 6,
        out_specs=(anywhere,) * 3,
        scratch_shapes=[
            vmem((LEV * ROWS, CELLS), F32), vmem((ROWS, CELLS), F32), vmem((HOT_ROWS, TILES * SLOTS), BF16),
            vmem((TILES * SLOTS, CELLS), F32), vmem((BLOCKS, CELLS), F32), vmem((BLOCKS, CELLS), jnp.int32),
            vmem((BLOCKS, CELLS), F32), pltpu.SemaphoreType.DMA((6,)), pltpu.SemaphoreType.DMA((3,)),
        ],
        compiler_params=pltpu.CompilerParams(vmem_limit_bytes=VMEM_BYTES),
    )(state, regrid, hot, drive.reshape(TILES * SLOTS, CELLS), dep, wet)
    return state.reshape(LEV, ROWS, CELLS), sea, regrid


def solution(mesh):
    both = P(("face", "tile"), None)
    return jax.shard_map(
        body,
        mesh=mesh,
        in_specs=(
            P(None, "face", "tile"), P("face", "tile"), P(), P(("face", "tile")),
            P(("face", "tile"), None, None), both, both, P(),
        ),
        out_specs=(P(None, "face", "tile"), both, P("face", "tile")),
        check_vma=False,
    )
```
